32 devices in a mesh: groups: 2 (over y), ep: 4 (over x, core), sub: 4 (over z).
Axes of the slice: x: 2, y: 2, z: 4, core: 2. Of those that a mesh axis runs over, the one named last changes fastest.
Arguments:
- row_codes: bfloat16 [2, 256, 7168], P(None, ('groups', 'ep', 'sub')), parts along dimension 1, may hold values from -6 to 6
- row_scales: float32 [2, 256, 56], P(None, ('groups', 'ep', 'sub')), parts along dimension 1, may hold values from 0.3 to 3
- expert_ids: int32 [2, 256, 2], P(None, ('groups', 'ep', 'sub')), parts along dimension 1, may hold values from 0 to 3, all different within a row; in each aligned block of 8 rows (0 to 7, 8 to 15, ..., all dimensions but the last counted through in order) at most 5 rows name the same one
- gate_codes: int32 [2, 256, 2], P(None, ('groups', 'ep', 'sub')), parts along dimension 1, may hold values from 1 to 1023
- w_gate: bfloat16 [4, 7168, 2048], P('ep', None, 'sub'), may hold values from -0.0625 to 0.0625
- w_up: bfloat16 [4, 7168, 2048], P('ep', None, 'sub'), may hold values from -0.0625 to 0.0625
- w_down: bfloat16 [4, 2048, 7168], P('ep', 'sub'), may hold values from -0.125 to 0.125
Outputs:
- combined: bfloat16 [2, 256, 7168], P(None, ('groups', 'ep', 'sub')), parts along dimension 1
The draws below stay inside these ranges and needn't reach their ends.
There are 2 independent parts, one for each index of `groups`. The reference program is written for one: setup_inputs(seed, part) draws one part's arguments, and reference() takes and returns one part's arrays. A program takes and returns all parts, laid end to end along the dimension named above; an argument that names none is the same for every part. Nothing has to cross between parts.
Inputs may be any that keep to these rules, and one draw needn't show every extreme that they name: `expert_ids`: each row names 2 different experts. In each step no expert is named by more than 5 of one device's 8 rows, and in every draw some expert is named by exactly 5 rows of one device.
All inputs are finite; a program needn't handle non-finite values.
Results may differ from the reference program's by a relative error of at most 0.012.
Values may be sent and summed in bfloat16 or wider, within the bound.
No kernel may reach another device: no remote copies, remote signals or barrier semaphores. Data moves between devices by JAX's collectives and lax.ppermute only.
A program may use at most 128 MiB of HBM per device.

```python
import math
import jax
import jax.numpy as jnp
import numpy as np
from jax import lax

D = 7168
FF = 2048
SCALE_BLOCK = 128
TOP = 2
STEPS = 2
ROWS_DEV = 8
EXPERTS = 4
ROWS = 128
CAP = 5
N_EP = 4
N_SUB = 4


def with_ends(entries, own_key, low, largest):
    extent = entries.shape
    spot = [jax.random.randint(jax.random.fold_in(own_key, axis), (), 0, extent[axis]) for axis in range(len(extent))]
    entries = entries.at[tuple(spot)].set(low)
    longest = extent.index(max(extent))
    spot[longest] = (spot[longest] + 1) % extent[longest]
    return entries.at[tuple(spot)].set(largest)


def block_scale(own_key, extent, cuts, low, largest):
    def one(position, blocks):
        draws = jax.random.uniform(jax.random.fold_in(jax.random.fold_in(own_key, 6), position), (blocks,), jnp.float32, low / len(cuts), largest / len(cuts))
        return jnp.repeat(jnp.exp(draws), extent[position] // blocks).reshape((-1,) + (1,) * (len(extent) - position - 1))

    gain = one(*cuts[0])
    for cut in cuts[1:]:
        gain = gain * one(*cut)
    return gain


def deal_out(stream_key, own, number, rows, amount, top, bound, slope):
    order = jax.random.permutation(stream_key, amount)
    crowded, common = load_shares(amount, rows * top, bound, slope, True), load_shares(amount, rows * top, bound, slope, False)
    places = jnp.arange(amount)

    def named(sizes, offset_by):
        used = int((sizes > 0).sum())
        fixed = max(1, used // 4)
        shifted = fixed + (places - fixed + offset_by * (used - fixed)) % max(1, amount - fixed)
        return jnp.zeros((amount,), jnp.int32).at[order[jnp.where(places < fixed, places, shifted)]].set(jnp.asarray(sizes, jnp.int32))

    sizes = jnp.where(number % 4 == 0, named(crowded, number // 4), named(common, number - number // 4 - 1))
    mixed = jax.random.permutation(jax.random.fold_in(own, 3), amount)
    source_of, taker = mixed[0:amount // 2 * 2:2], mixed[1:amount // 2 * 2:2]
    margin = jnp.minimum(sizes[source_of] - 1, bound - sizes[taker]) // 2
    margin = jnp.where((source_of == order[0]) | (taker == order[0]) | (sizes[taker] == 0), 0, jnp.maximum(margin, 0))
    shifted = jax.random.randint(jax.random.fold_in(own, 4), (amount // 2,), 0, 1 << 20) % (margin + 1)
    sizes = sizes.at[source_of].add(-shifted).at[taker].add(shifted)
    labels = jnp.searchsorted(jnp.cumsum(sizes), jnp.arange(rows * top), side="right").astype(jnp.int32)
    listing = labels.reshape(top, rows).T
    listing = listing[jax.random.permutation(jax.random.fold_in(own, 1), rows)]
    offset_by = jax.random.randint(jax.random.fold_in(own, 2), (rows, 1), 0, top)
    return jnp.take_along_axis(listing, (jnp.arange(top)[None, :] + offset_by) % top, axis=1)


def load_shares(amount, total, most, slope, full):
    loads = [(1 << 20) // math.isqrt(rank ** slope) + 1 for rank in range(1, amount + 1)]
    largest = most if full else min(most, max(-(-total // amount), total * loads[0] // sum(loads)))
    least = 1 if total - largest >= amount - 1 else 0
    counts, surplus = [largest] + [least] * (amount - 1), total - largest - least * (amount - 1)
    while surplus > 0:
        free = [i for i in range(1, amount) if counts[i] < largest] or [i for i in range(1, amount) if counts[i] < most]
        whole, remaining = sum([loads[i] for i in free]), surplus
        for i in free:
            extra = min(most - counts[i], max(1, remaining * loads[i] // whole), surplus)
            counts[i] = counts[i] + extra
            surplus = surplus - extra
    return np.array(counts)


def bell_draw(own_key, shape, spread, bound, split=(), kind=jnp.bfloat16):
    values = spread * jax.random.normal(own_key, shape, jnp.float32)
    if split:
        values = values * block_scale(own_key, shape, split, -0.22, 0.18)
    return jnp.clip(values, -bound, bound).astype(kind)


def setup_inputs(seed: int = 0, part: int = 0) -> dict:
    seeds = jax.random.split(jax.random.key(seed), 8)
    part_splits = jax.random.split(jax.random.fold_in(seeds[7], part), 8)
    row_codes = bell_draw(part_splits[0], (STEPS, ROWS, D), 1.0, 6.0, ((1, 16),))
    row_scales = jnp.clip(jnp.exp(math.log(3.0) - 2.3025851 * jax.random.uniform(part_splits[1], (STEPS, ROWS, D // SCALE_BLOCK), jnp.float32) ** block_scale(part_splits[1], (STEPS, ROWS, D // SCALE_BLOCK), ((1, 16),), -0.2, 0.2)), 0.3, 3.0)
    expert_ids_keys = jax.random.split(jax.random.fold_in(part_splits[2], 1), STEPS * ROWS // ROWS_DEV)
    expert_ids_turns = jax.random.permutation(jax.random.fold_in(part_splits[2], 3), STEPS * ROWS // ROWS_DEV)
    expert_ids = jax.vmap(lambda own, number: deal_out(jax.random.fold_in(part_splits[2], 2), own, number, ROWS_DEV, EXPERTS, TOP, CAP, 2))(expert_ids_keys, expert_ids_turns).reshape((STEPS, ROWS, TOP))
    gate_codes = with_ends(jax.random.randint(part_splits[3], (STEPS, ROWS, TOP), 1, 1024), jax.random.fold_in(part_splits[3], 1), 1, 1023).astype(jnp.int32)
    w_gate = bell_draw(seeds[4], (EXPERTS, D, FF), D ** -0.5, 0.0625, ((0, 4), (2, 4)))
    w_up = bell_draw(seeds[5], (EXPERTS, D, FF), D ** -0.5, 0.0625, ((0, 4), (2, 4)))
    w_down = bell_draw(seeds[6], (EXPERTS, FF, D), FF ** -0.5, 0.125, ((0, 4), (1, 4)))
    return {"row_codes": row_codes, "row_scales": row_scales, "expert_ids": expert_ids, "gate_codes": gate_codes, "w_gate": w_gate, "w_up": w_up, "w_down": w_down}


routed_scale = 2.5


def dequantize(codes, scales):
    blocks = codes.astype(jnp.float32).reshape(codes.shape[0], -1, SCALE_BLOCK)
    scaled = blocks * scales[:, :, None]
    return scaled.reshape(codes.shape[0], -1).astype(jnp.bfloat16)


def reference(row_codes, row_scales, expert_ids, gate_codes, w_gate, w_up, w_down):
    most_slots = N_EP * N_SUB * CAP
    results = []
    for step_index in range(STEPS):
        tokens = dequantize(row_codes[step_index], row_scales[step_index])
        codes_f = gate_codes[step_index].astype(jnp.float32)
        total = jnp.sum(codes_f, axis=1, keepdims=True)
        weights = (routed_scale * codes_f) / total
        flat_ids = expert_ids[step_index].reshape(-1)
        flat_weights = weights.reshape(-1)

        def one_expert(packed):
            expert, gate_mat, up_mat, down_mat = packed
            chosen = flat_ids == expert
            picked = jnp.nonzero(chosen, size=most_slots, fill_value=0)[0].astype(jnp.int32)
            valid = jnp.arange(most_slots, dtype=jnp.int32) < jnp.sum(chosen.astype(jnp.int32))
            row_index = (picked // TOP).astype(jnp.int32)
            inputs = tokens[row_index]
            gate_value = jnp.dot(inputs, gate_mat, preferred_element_type=jnp.float32)
            up_value = jnp.dot(inputs, up_mat, preferred_element_type=jnp.float32)
            hidden = (jax.nn.silu(gate_value) * up_value).astype(jnp.bfloat16)
            hidden_blocks = hidden.astype(jnp.float32).reshape(most_slots, N_SUB, FF // N_SUB)
            down_blocks = down_mat.astype(jnp.float32).reshape(N_SUB, FF // N_SUB, D)
            partial_out = jnp.einsum("nsf,sfd->nsd", hidden_blocks, down_blocks, precision=lax.Precision.HIGHEST)
            expert_out = partial_out.astype(jnp.bfloat16).astype(jnp.float32).sum(axis=1).astype(jnp.bfloat16)
            scale_rows = jnp.where(valid, flat_weights[picked], jnp.float32(0.0))
            return row_index, scale_rows[:, None] * expert_out.astype(jnp.float32)

        row_lists, contribs = lax.map(one_expert, (jnp.arange(EXPERTS, dtype=jnp.int32), w_gate, w_up, w_down))
        summed = jnp.zeros((ROWS, D), jnp.float32).at[row_lists.reshape(-1)].add(contribs.reshape(-1, D))
        results.append(summed.astype(jnp.bfloat16))
    return jnp.stack(results)
```

```python
import jax
import jax.numpy as jnp
from jax import lax
from jax.sharding import PartitionSpec as P

routed_scale = 2.5
chunk_count = 4


def bits_of(count):
    return [1 << b for b in reversed(range(count.bit_length() - 1))]


def swap(value, axis_name, bit):
    count = lax.axis_size(axis_name)
    return lax.ppermute(value, axis_name, [(i, i ^ bit) for i in range(count)])


def dequantize(codes, scales):
    block_size = codes.shape[1] // scales.shape[1]
    blocks = codes.astype(jnp.float32).reshape(codes.shape[0], -1, block_size)
    scaled = blocks * scales[:, :, None]
    return scaled.reshape(codes.shape[0], -1).astype(jnp.bfloat16)


def route_columns(chosen_ids, codes, ep_count):
    experts = jnp.arange(ep_count, dtype=jnp.int32)
    dense = jnp.sum(jnp.where(chosen_ids[:, :, None] == experts, codes[:, :, None], 0), axis=1)
    both = jnp.concatenate([dense // 16 * 16, dense % 16], axis=1).astype(jnp.bfloat16)
    return jnp.pad(both, ((0, 0), (0, -both.shape[1] % 128)))


def body(row_codes, row_scales, expert_ids, gate_codes, w_gate, w_up, w_down):
    ep_count = lax.axis_size("ep")
    sub_count = lax.axis_size("sub")
    steps_here, row_count, features = row_codes.shape
    rows = steps_here * row_count
    stages = [("sub", b) for b in bits_of(sub_count)] + [("ep", b) for b in bits_of(ep_count)]
    tokens = dequantize(row_codes.reshape(rows, features), row_scales.reshape(rows, -1))
    codes = route_columns(expert_ids.reshape(rows, -1), gate_codes.reshape(rows, -1), ep_count)
    width = features // chunk_count
    parts = []
    for k in range(chunk_count):
        part = tokens[:, k * width : (k + 1) * width]
        parts.append(jnp.concatenate([part, codes], axis=1) if k == 0 else part)
    gathered = []
    for part in parts:
        for axis_name, bit in stages:
            part = jnp.concatenate([part, swap(part, axis_name, bit)], axis=0)
        gathered.append(part)
    me = lax.axis_index("ep")
    sent = gathered[0][:, width : width + 2 * ep_count].astype(jnp.float32)
    dense = sent[:, :ep_count] + sent[:, ep_count:]
    total = jnp.sum(dense, axis=1, keepdims=True)
    mine = jnp.sum(jnp.where(jnp.arange(ep_count) == me, dense, 0.0), axis=1, keepdims=True)
    weight = routed_scale * mine / total
    gate_value = up_value = 0.0
    for k, part in enumerate(gathered):
        inputs = part[:, :width]
        span = slice(k * width, (k + 1) * width)
        gate_value += jnp.dot(inputs, w_gate[0, span], preferred_element_type=jnp.float32)
        up_value += jnp.dot(inputs, w_up[0, span], preferred_element_type=jnp.float32)
    hidden = (jax.nn.silu(gate_value) * up_value).astype(jnp.bfloat16)
    results = []
    for k in range(chunk_count):
        span = slice(k * width, (k + 1) * width)
        held = jnp.dot(hidden, w_down[0, :, span], preferred_element_type=jnp.float32)
        held = (held * weight).astype(jnp.bfloat16)
        for axis_name, bit in reversed(stages):
            half = held.shape[0] // 2
            came = swap(held[half:], axis_name, bit)
            held = held[:half].astype(jnp.float32) + came.astype(jnp.float32)
            held = held.astype(jnp.bfloat16)
        results.append(held)
    return jnp.concatenate(results, axis=1).reshape(steps_here, row_count, features)


def solution(mesh):
    rows = P(None, ("groups", "ep", "sub"), None)
    return jax.shard_map(
        body,
        mesh=mesh,
        in_specs=(rows, rows, rows, rows, P("ep", None, "sub"), P("ep", None, "sub"), P("ep", "sub", None)),
        out_specs=rows,
        check_vma=False,
    )
```

```python
import jax
import jax.numpy as jnp
from jax import lax
from jax.sharding import PartitionSpec as P

routed_scale = 2.5
column_parts = 2


def bits_of(count):
    return [1 << b for b in reversed(range(count.bit_length() - 1))]


def swap(value, axis_name, bit):
    count = lax.axis_size(axis_name)
    return lax.ppermute(value, axis_name, [(i, i ^ bit) for i in range(count)])


def after(value, *others):
    return lax.optimization_barrier((value, *others))[0] if others else value


def join(*parts):
    return jnp.concatenate(parts, axis=0)


def add_up(*terms):
    total = terms[0].astype(jnp.float32)
    for term in terms[1:]:
        total = total + term.astype(jnp.float32)
    return total


def dequantize(codes, scales):
    block_size = codes.shape[1] // scales.shape[1]
    blocks = codes.astype(jnp.float32).reshape(codes.shape[0], -1, block_size)
    scaled = blocks * scales[:, :, None]
    return scaled.reshape(codes.shape[0], -1).astype(jnp.bfloat16)


def route_columns(chosen_ids, codes, ep_count):
    experts = jnp.arange(ep_count, dtype=jnp.int32)
    dense = jnp.sum(jnp.where(chosen_ids[:, :, None] == experts, codes[:, :, None], 0), axis=1)
    both = jnp.concatenate([dense // 16 * 16, dense % 16], axis=1).astype(jnp.bfloat16)
    return jnp.pad(both, ((0, 0), (0, -both.shape[1] % 128)))


def body(row_codes, row_scales, expert_ids, gate_codes, w_gate, w_up, w_down):
    ep_count = lax.axis_size("ep")
    sub_bits = bits_of(lax.axis_size("sub"))
    ep_bits = bits_of(ep_count)
    steps_here, rows, features = row_codes.shape
    width = features // column_parts
    tokens = dequantize(row_codes.reshape(-1, features), row_scales.reshape(steps_here * rows, -1))
    codes = route_columns(expert_ids.reshape(steps_here * rows, -1), gate_codes.reshape(steps_here * rows, -1), ep_count)
    tokens = jnp.concatenate([codes, tokens], axis=1)
    extra = codes.shape[1]
    crossed = swap(tokens, "ep", ep_bits[0])
    me = lax.axis_index("ep")
    first = None
    own_gives = []
    waiting = []
    step_done = []
    returned = []
    for step in range(steps_here):
        gate_value = up_value = 0.0
        for k in range(column_parts):
            low = 0 if k == 0 else extra + k * width
            block = (slice(step * rows, (step + 1) * rows), slice(low, extra + (k + 1) * width))
            own = tokens[block]
            part = own
            for n, bit in enumerate(sub_bits):
                if n == 0 and first is not None:
                    part = after(part, first)
                came = swap(part, "sub", bit)
                if first is None:
                    first = came
                part = join(part, came)
            part = join(part, crossed[block], swap(part[rows:], "ep", ep_bits[0]))
            for bit in ep_bits[1:]:
                part = after(part, *step_done)
                part = join(part, swap(part, "ep", bit))
            if k == 0:
                sent = part[:, : 2 * ep_count].astype(jnp.float32)
                dense = sent[:, :ep_count] + sent[:, ep_count:]
                total = jnp.sum(dense, axis=1, keepdims=True)
                mine = jnp.sum(jnp.where(jnp.arange(ep_count) == me, dense, 0.0), axis=1, keepdims=True)
                weight = routed_scale * mine / total
            inputs = part[:, extra - low :] if k == 0 else part
            span = slice(k * width, (k + 1) * width)
            gate_value += jnp.dot(inputs, w_gate[0, span], preferred_element_type=jnp.float32)
            up_value += jnp.dot(inputs, w_up[0, span], preferred_element_type=jnp.float32)
        hidden = (jax.nn.silu(gate_value) * up_value).astype(jnp.bfloat16)
        step_done = []
        for k in range(column_parts):
            span = slice(k * width, (k + 1) * width)
            held = jnp.dot(hidden, w_down[0, :, span], preferred_element_type=jnp.float32)
            held = (held * weight).astype(jnp.bfloat16)
            step_done.append(held)
            for bit in reversed(ep_bits[1:]):
                half = held.shape[0] // 2
                held = add_up(held[:half], swap(held[half:], "ep", bit)).astype(jnp.bfloat16)
            half = held.shape[0] // 2
            give = held[half + rows :]
            if len(waiting) >= 3:
                give = after(give, waiting[-3])
            own_gives.append(held[half : half + rows])
            own = [held[:rows]]
            rest = add_up(held[rows:half], swap(give, "ep", ep_bits[0])).astype(jnp.bfloat16)
            for n, bit in enumerate(reversed(sub_bits)):
                half = (rest.shape[0] + rows) // 2
                came = swap(rest[half - rows :], "sub", bit)
                if n == 0:
                    waiting.append(came)
                own.append(came[:rows])
                if half > rows:
                    rest = add_up(rest[: half - rows], came[rows:]).astype(jnp.bfloat16)
            returned.append(own)
    by_step = [own_gives[s * column_parts : (s + 1) * column_parts] for s in range(steps_here)]
    crossed = swap(join(*[jnp.concatenate(gives, axis=1) for gives in by_step]), "ep", ep_bits[0])
    results = []
    for step in range(steps_here):
        outs = []
        for k in range(column_parts):
            own = returned[step * column_parts + k]
            block = (slice(step * rows, (step + 1) * rows), slice(k * width, (k + 1) * width))
            outs.append(add_up(*own, crossed[block]).astype(jnp.bfloat16))
        results.append(jnp.concatenate(outs, axis=1))
    return jnp.stack(results)


def solution(mesh):
    rows = P(None, ("groups", "ep", "sub"), None)
    return jax.shard_map(
        body,
        mesh=mesh,
        in_specs=(rows, rows, rows, rows, P("ep", None, "sub"), P("ep", None, "sub"), P("ep", "sub", None)),
        out_specs=rows,
        check_vma=False,
    )
```

```python
import functools

import jax
import jax.numpy as jnp
from jax import lax
from jax.experimental import pallas as pl
from jax.experimental.pallas import tpu as pltpu
from jax.sharding import PartitionSpec as P

routed_scale = 2.5
column_parts = 2
F_Z2 = 2
F_XORD = 1
F_C1 = 1
F_RLAG = 0
F_Z2R = 2
F_CHOLD = 1


def bits_of(count):
    return [1 << b for b in reversed(range(count.bit_length() - 1))]


def swap(value, axis_name, bit):
    count = lax.axis_size(axis_name)
    return lax.ppermute(value, axis_name, [(i, i ^ bit) for i in range(count)])


def after(value, *others):
    return lax.optimization_barrier((value, *others))[0] if others else value


def join(*parts):
    return jnp.concatenate(parts, axis=0)


def add_up(*terms):
    total = terms[0].astype(jnp.float32)
    for term in terms[1:]:
        total = total + term.astype(jnp.float32)
    return total


def prepare_kernel(ep_count, extra, width, codes_ref, scales_ref, ids_ref, gates_ref, all_ref, *part_refs):
    steps_here, rows, features = codes_ref.shape
    blocks = scales_ref.shape[2]
    size = features // blocks
    lane = lax.broadcasted_iota(jnp.int32, (rows, extra), 1)
    expert = lax.rem(lane, ep_count)
    whole = [[], []]
    for step in range(steps_here):
        ids, gates = ids_ref[step], gates_ref[step]
        code = jnp.zeros((rows, extra), jnp.int32)
        for route in range(ids.shape[1]):
            here = jnp.broadcast_to(ids[:, route : route + 1], (rows, extra)) == expert
            code += jnp.where(here, jnp.broadcast_to(gates[:, route : route + 1], (rows, extra)), 0)
        low = code & 15
        sent = jnp.where(lane < ep_count, code - low, jnp.where(lane < 2 * ep_count, low, 0))
        pieces = [sent.astype(jnp.float32)]
        scales = scales_ref[step]
        codes = codes_ref[step].astype(jnp.float32)
        for b in range(blocks):
            pieces.append(codes[:, b * size : (b + 1) * size] * jnp.broadcast_to(scales[:, b : b + 1], (rows, size)))
        row = jnp.concatenate(pieces, axis=1)
        whole[step % 2].append(row)
        count = (features // width)
        for k in range(count):
            low_at = 0 if k == 0 else extra + k * width
            part_refs[step * count + k][...] = row[:, low_at : extra + (k + 1) * width].astype(jnp.bfloat16)
    every = [row for pair in zip(*whole) for row in pair]
    all_ref[...] = jnp.concatenate(every, axis=0).astype(jnp.bfloat16)


def prepare(row_codes, row_scales, expert_ids, gate_codes, ep_count, width):
    steps_here, rows, features = row_codes.shape
    extra = -(-2 * ep_count // 128) * 128
    count = features // width
    shapes = [jax.ShapeDtypeStruct((steps_here * rows, features + extra), jnp.bfloat16)]
    for step in range(steps_here):
        for k in range(count):
            shapes.append(jax.ShapeDtypeStruct((rows, width + (extra if k == 0 else 0)), jnp.bfloat16))
    outs = pl.pallas_call(
        functools.partial(prepare_kernel, ep_count, extra, width),
        out_shape=shapes,
        compiler_params=pltpu.CompilerParams(vmem_limit_bytes=16 << 20),
    )(row_codes, row_scales, expert_ids, gate_codes)
    return outs[0], outs[1:], extra


def body(row_codes, row_scales, expert_ids, gate_codes, w_gate, w_up, w_down):
    ep_count = lax.axis_size("ep")
    sub_bits = bits_of(lax.axis_size("sub"))
    ep_bits = bits_of(ep_count)
    steps_here, rows, features = row_codes.shape
    width = features // column_parts
    tokens, owns, extra = prepare(row_codes, row_scales, expert_ids, gate_codes, ep_count, width)
    crossed = swap(tokens, "ep", ep_bits[0])
    me = lax.axis_index("ep")
    z2s, z1s, xs = [], [], []
    own_gives = []
    waiting = []
    step_done, core_back = [], []
    returned = []
    gathered = []
    for step in range(steps_here):
        for k in range(column_parts):
            c = step * column_parts + k
            low = 0 if k == 0 else extra + k * width
            block = (slice(step * rows, (step + 1) * rows), slice(low, extra + (k + 1) * width))
            part = owns[c]
            for n, bit in enumerate(sub_bits):
                if n == 0:
                    if F_Z2 == 0 and c >= 1:
                        part = after(part, z2s[0])
                    if F_Z2 == 1 and c >= 2:
                        part = after(part, z1s[0])
                    if F_Z2 == 2 and c >= 2:
                        part = after(part, z2s[1])
                    if F_Z2 == 3 and c >= 2:
                        part = after(part, z2s[0])
                came = swap(part, "sub", bit)
                if n == 0:
                    z2s.append(came)
                if n == 1:
                    z1s.append(came)
                part = join(part, came)
            give = part[rows:]
            if F_XORD and c >= 2:
                give = after(give, xs[c - 2])
            xs.append(swap(give, "ep", ep_bits[0]))
            part = join(part, crossed[block], xs[-1])
            gathered.append((part, low))
    for step in range(steps_here):
        gate_value = up_value = 0.0
        for k in range(column_parts):
            part, low = gathered[step * column_parts + k]
            for bit in ep_bits[1:]:
                if F_C1:
                    part = after(part, *step_done)
                part = join(part, swap(part, "ep", bit))
            if F_CHOLD and core_back:
                part = after(part, *core_back)
            if k == 0:
                sent = part[:, : 2 * ep_count].astype(jnp.float32)
                dense = sent[:, :ep_count] + sent[:, ep_count:]
                total = jnp.sum(dense, axis=1, keepdims=True)
                mine = jnp.sum(jnp.where(jnp.arange(ep_count) == me, dense, 0.0), axis=1, keepdims=True)
                weight = routed_scale * mine / total
            inputs = part[:, extra - low :] if k == 0 else part
            span = slice(k * width, (k + 1) * width)
            gate_value += jnp.dot(inputs, w_gate[0, span], preferred_element_type=jnp.float32)
            up_value += jnp.dot(inputs, w_up[0, span], preferred_element_type=jnp.float32)
        hidden = (jax.nn.silu(gate_value) * up_value).astype(jnp.bfloat16)
        step_done = []
        core_back = []
        for k in range(column_parts):
            span = slice(k * width, (k + 1) * width)
            held = jnp.dot(hidden, w_down[0, :, span], preferred_element_type=jnp.float32)
            held = (held * weight).astype(jnp.bfloat16)
            step_done.append(held)
            for bit in reversed(ep_bits[1:]):
                half = held.shape[0] // 2
                held = add_up(held[:half], swap(held[half:], "ep", bit)).astype(jnp.bfloat16)
            core_back.append(held)
            returned.append(held)
    finals = []
    for c, held in enumerate(returned):
        half = held.shape[0] // 2
        give = held[half + rows :]
        if F_RLAG and len(waiting) >= F_RLAG:
            give = after(give, waiting[-F_RLAG])
        own_gives.append(held[half : half + rows])
        own = [held[:rows]]
        rest = add_up(held[rows:half], swap(give, "ep", ep_bits[0])).astype(jnp.bfloat16)
        for n, bit in enumerate(reversed(sub_bits)):
            half = (rest.shape[0] + rows) // 2
            give = rest[half - rows :]
            if F_Z2R == 1 and n == 1 and c == 0:
                give = after(give, *returned[2:])
            if F_Z2R == 2 and n == 0 and c == 0:
                give = after(give, *returned[2:])
            came = swap(give, "sub", bit)
            if n == 0:
                waiting.append(came)
            own.append(came[:rows])
            if half > rows:
                rest = add_up(rest[: half - rows], came[rows:]).astype(jnp.bfloat16)
        finals.append(own)
    by_step = [own_gives[s * column_parts : (s + 1) * column_parts] for s in range(steps_here)]
    crossed = swap(join(*[jnp.concatenate(gives, axis=1) for gives in by_step]), "ep", ep_bits[0])
    results = []
    for step in range(steps_here):
        outs = []
        for k in range(column_parts):
            own = finals[step * column_parts + k]
            block = (slice(step * rows, (step + 1) * rows), slice(k * width, (k + 1) * width))
            outs.append(add_up(*own, crossed[block]).astype(jnp.bfloat16))
        results.append(jnp.concatenate(outs, axis=1))
    return jnp.stack(results)


def solution(mesh):
    rows = P(None, ("groups", "ep", "sub"), None)
    return jax.shard_map(
        body,
        mesh=mesh,
        in_specs=(rows, rows, rows, rows, P("ep", None, "sub"), P("ep", None, "sub"), P("ep", "sub", None)),
        out_specs=rows,
        check_vma=False,
    )
```

```python
import functools

import jax
import jax.numpy as jnp
from jax import lax
from jax.experimental import pallas as pl
from jax.experimental.pallas import tpu as pltpu
from jax.sharding import PartitionSpec as P

routed_scale = 2.5
column_parts = 2
F_Z2 = 2
F_XORD = 1
F_C1 = 1
F_Z2R = 2
F_CHOLD = 1
F_OUT1 = 2
F_FIN0 = 1
F_OWN0 = 0
F_LATE = 1
F_SPLIT1 = 1
F_BACK0 = 2


def bits_of(count):
    return [1 << b for b in reversed(range(count.bit_length() - 1))]


def swap(value, axis_name, bit):
    count = lax.axis_size(axis_name)
    return lax.ppermute(value, axis_name, [(i, i ^ bit) for i in range(count)])


def after(value, *others):
    return lax.optimization_barrier((value, *others))[0] if others else value


def join(*parts):
    return jnp.concatenate(parts, axis=0)


def add_up(*terms):
    total = terms[0].astype(jnp.float32)
    for term in terms[1:]:
        total = total + term.astype(jnp.float32)
    return total


def prepare_kernel(ep_count, extra, cuts, codes_hbm, scales_hbm, ids_hbm, gates_hbm, all_ref, *refs):
    part_refs, (codes_ref, scales_ref, ids_ref, gates_ref, sems) = refs[:-5], refs[-5:]
    moves = []
    for n, (source, target) in enumerate(
        [(codes_hbm, codes_ref), (scales_hbm, scales_ref), (ids_hbm, ids_ref), (gates_hbm, gates_ref)]
    ):
        moves.append(pltpu.make_async_copy(source, target, sems.at[n]))
        moves[-1].start()
    for move in moves:
        move.wait()
    steps_here, rows, features = codes_ref.shape
    blocks = scales_ref.shape[2]
    size = features // blocks
    lane = lax.broadcasted_iota(jnp.int32, (rows, extra), 1)
    expert = lax.rem(lane, ep_count)
    diagonal = lax.broadcasted_iota(jnp.int32, (rows, rows), 0) == lax.broadcasted_iota(jnp.int32, (rows, rows), 1)

    def column(values):
        spread = jnp.broadcast_to(values.astype(jnp.float32), (rows, rows))
        total = jnp.sum(jnp.where(diagonal, spread, 0.0), axis=1, keepdims=True)
        return jnp.broadcast_to(total.astype(jnp.int32), (rows, extra))

    every = []
    target = 0
    for step in range(steps_here):
        ids, gates = ids_ref[step], gates_ref[step]
        code = jnp.zeros((rows, extra), jnp.int32)
        for route in range(ids.shape[0]):
            code += jnp.where(column(ids[route : route + 1]) == expert, column(gates[route : route + 1]), 0)
        low = code & 15
        sent = jnp.where(lane < ep_count, code - low, jnp.where(lane < 2 * ep_count, low, 0))
        pieces = [sent.astype(jnp.float32)]
        scales = scales_ref[step]
        codes = codes_ref[step].astype(jnp.float32)
        for b in range(blocks):
            pieces.append(codes[:, b * size : (b + 1) * size] * jnp.broadcast_to(scales[:, b : b + 1], (rows, size)))
        row = jnp.concatenate(pieces, axis=1)
        every.append(row)
        for start, end in spans_of(features, cuts[step], extra):
            part_refs[target][...] = row[:, start:end].astype(jnp.bfloat16)
            target += 1
    all_ref[...] = jnp.concatenate(every, axis=0).astype(jnp.bfloat16)


def spans_of(features, count, extra):
    width = features // count
    return [(extra + k * width if k else 0, extra + (k + 1) * width) for k in range(count)]


def prepare(row_codes, row_scales, expert_ids, gate_codes, ep_count, cuts):
    steps_here, rows, features = row_codes.shape
    extra = -(-2 * ep_count // 128) * 128
    shapes = [jax.ShapeDtypeStruct((steps_here * rows, features + extra), jnp.bfloat16)]
    for step in range(steps_here):
        for start, end in spans_of(features, cuts[step], extra):
            shapes.append(jax.ShapeDtypeStruct((rows, end - start), jnp.bfloat16))
    ins = [row_codes, row_scales, expert_ids.transpose(0, 2, 1), gate_codes.transpose(0, 2, 1)]
    outs = pl.pallas_call(
        functools.partial(prepare_kernel, ep_count, extra, cuts),
        out_shape=shapes,
        in_specs=[pl.BlockSpec(memory_space=pl.ANY)] * len(ins),
        scratch_shapes=[pltpu.VMEM(v.shape, v.dtype) for v in ins] + [pltpu.SemaphoreType.DMA((len(ins),))],
    )(*ins)
    return outs[0], outs[1:], extra


def body(row_codes, row_scales, expert_ids, gate_codes, w_gate, w_up, w_down):
    ep_count = lax.axis_size("ep")
    sub_bits = bits_of(lax.axis_size("sub"))
    ep_bits = bits_of(ep_count)
    steps_here, rows, features = row_codes.shape
    out_cuts = [column_parts] + [F_OUT1] * (steps_here - 1)
    back_cuts = [F_BACK0] + [column_parts] * (steps_here - 1)
    tokens, owns, extra = prepare(row_codes, row_scales, expert_ids, gate_codes, ep_count, out_cuts)
    crossed = swap(tokens, "ep", ep_bits[0])
    me = lax.axis_index("ep")
    far, near, xs = [], [], []
    gathered = []
    for step in range(steps_here):
        parts = []
        for k, (start, end) in enumerate(spans_of(features, out_cuts[step], extra)):
            part = owns[len(xs)]
            for n, bit in enumerate(sub_bits):
                if n == 0 and step >= 1 and F_Z2 == 1:
                    part = after(part, near[0])
                if n == 0 and step >= 1 and F_Z2 == 2:
                    part = after(part, far[1])
                if n == 0 and step >= 1 and F_Z2 == 3:
                    part = after(part, far[0])
                came = swap(part, "sub", bit)
                if n == 0:
                    far.append(came)
                if n == 1:
                    near.append(came)
                part = join(part, came)
            give = part[rows:]
            if F_XORD and step >= 1:
                give = after(give, xs[F_XORD - 1])
            xs.append(swap(give, "ep", ep_bits[0]))
            parts.append((part, crossed[step * rows : (step + 1) * rows, start:end], xs[-1]))
        gathered.append(parts)
    step_done, core_back = [], []
    returned = []
    for step in range(steps_here):
        gate_value = up_value = 0.0
        for part, (start, end) in zip(gathered[step], spans_of(features, out_cuts[step], extra)):
            part, came_own, came_rest = part
            if F_LATE and step_done:
                came_rest = after(came_rest, *step_done)
            part = join(part, came_own, came_rest)
            for bit in ep_bits[1:]:
                part = after(part, *step_done) if F_C1 else part
                part = join(part, swap(part, "ep", bit))
            part = after(part, *core_back) if F_CHOLD else part
            if start == 0:
                sent = part[:, : 2 * ep_count].astype(jnp.float32)
                dense = sent[:, :ep_count] + sent[:, ep_count:]
                total = jnp.sum(dense, axis=1, keepdims=True)
                mine = jnp.sum(jnp.where(jnp.arange(ep_count) == me, dense, 0.0), axis=1, keepdims=True)
                weight = routed_scale * mine / total
                part = part[:, extra:]
            span = slice(max(start - extra, 0), end - extra)
            gate_value += jnp.dot(part, w_gate[0, span], preferred_element_type=jnp.float32)
            up_value += jnp.dot(part, w_up[0, span], preferred_element_type=jnp.float32)
        hidden = (jax.nn.silu(gate_value) * up_value).astype(jnp.bfloat16)
        step_done = []
        core_back = []
        for start, end in spans_of(features, back_cuts[step], 0):
            held = jnp.dot(hidden, w_down[0, :, start:end], preferred_element_type=jnp.float32)
            held = (held * weight).astype(jnp.bfloat16)
            step_done.append(held)
            for bit in reversed(ep_bits[1:]):
                half = held.shape[0] // 2
                held = add_up(held[:half], swap(held[half:], "ep", bit)).astype(jnp.bfloat16)
            core_back.append(held)
            returned.append((step, start, end, held))
    last = [held for step, _, _, held in returned if step == steps_here - 1]
    finals, own_gives, owns, restss, crossings = [], [], [], [], []
    for step in range(steps_here):
        split = rows if step >= F_OWN0 else 0
        own, rests, gives = [], [], []
        for _, start, end, held in [entry for entry in returned if entry[0] == step]:
            half = held.shape[0] // 2
            came = swap(held[half + split :], "ep", ep_bits[0])
            mine = [held[:rows]]
            if split:
                gives.append(held[half : half + rows])
            else:
                mine.append(came[:rows])
                came = came[rows:]
            crossings.append(came)
            rest = add_up(held[rows:half], came).astype(jnp.bfloat16)
            for n, bit in enumerate(reversed(sub_bits[1:])):
                half = (rest.shape[0] + rows) // 2
                give = rest[half - rows :]
                if step == 0 and n == 0 and F_Z2R == 2:
                    give = after(give, *last)
                came = swap(give, "sub", bit)
                mine.append(came[:rows])
                rest = add_up(rest[: half - rows], came[rows:]).astype(jnp.bfloat16)
            own.append(mine)
            rests.append(rest)
        owns.append(own)
        restss.append(rests)
        if split:
            own_gives.append(jnp.concatenate(gives, axis=1))
    for step in range(steps_here):
        own, rests = owns[step], restss[step]
        if step == 0 or not F_SPLIT1:
            give = jnp.concatenate(rests, axis=1)
            if step == 0 and F_Z2R == 1:
                give = after(give, *last)
            if step == 0 and F_Z2R == 3:
                give = after(give, crossings[back_cuts[0]])
            if step == 0 and F_Z2R == 4:
                give = after(give, crossings[-1])
            if step and F_FIN0:
                give = after(give, finals[step - 1])
            came = swap(give, "sub", sub_bits[0])
        else:
            came = jnp.concatenate([swap(give, "sub", sub_bits[0]) for give in rests], axis=1)
        own = jnp.concatenate([add_up(*mine) for mine in own], axis=1)
        finals.append(add_up(own, came) if step >= F_OWN0 else add_up(own, came).astype(jnp.bfloat16))
    crossed = swap(join(*own_gives), "ep", ep_bits[0])
    for n in range(len(own_gives)):
        step = steps_here - len(own_gives) + n
        finals[step] = add_up(finals[step], crossed[n * rows : (n + 1) * rows]).astype(jnp.bfloat16)
    return jnp.stack(finals)


def solution(mesh):
    rows = P(None, ("groups", "ep", "sub"), None)
    return jax.shard_map(
        body,
        mesh=mesh,
        in_specs=(rows, rows, rows, rows, P("ep", None, "sub"), P("ep", None, "sub"), P("ep", "sub", None)),
        out_specs=rows,
        check_vma=False,
    )
```

```python
import functools

import jax
import jax.numpy as jnp
from jax import lax
from jax.experimental import pallas as pl
from jax.experimental.pallas import tpu as pltpu
from jax.sharding import PartitionSpec as P

routed_scale = 2.5
column_parts = 2
F_Z2 = 2
F_XORD = 2
F_C1 = 1
F_Z2R = 2
F_CHOLD = 1
F_OUT1 = 2
F_FIN0 = 1
F_OWN0 = 0
F_LATE = 1
F_SPLIT1 = 1
F_BACK0 = 2


def bits_of(count):
    return [1 << b for b in reversed(range(count.bit_length() - 1))]


def swap(value, axis_name, bit):
    count = lax.axis_size(axis_name)
    return lax.ppermute(value, axis_name, [(i, i ^ bit) for i in range(count)])


def after(value, *others):
    return lax.optimization_barrier((value, *others))[0] if others else value


def join(*parts):
    return jnp.concatenate(parts, axis=0)


def add_up(*terms):
    total = terms[0].astype(jnp.float32)
    for term in terms[1:]:
        total = total + term.astype(jnp.float32)
    return total


def prepare_kernel(ep_count, extra, cuts, codes_hbm, scales_hbm, ids_hbm, gates_hbm, all_ref, *refs):
    part_refs, (codes_ref, scales_ref, ids_ref, gates_ref, sems) = refs[:-5], refs[-5:]
    moves = []
    for n, (source, target) in enumerate(
        [(codes_hbm, codes_ref), (scales_hbm, scales_ref), (ids_hbm, ids_ref), (gates_hbm, gates_ref)]
    ):
        moves.append(pltpu.make_async_copy(source, target, sems.at[n]))
        moves[-1].start()
    for move in moves:
        move.wait()
    steps_here, rows, features = codes_ref.shape
    blocks = scales_ref.shape[2]
    size = features // blocks
    lane = lax.broadcasted_iota(jnp.int32, (rows, extra), 1)
    expert = lax.rem(lane, ep_count)
    diagonal = lax.broadcasted_iota(jnp.int32, (rows, rows), 0) == lax.broadcasted_iota(jnp.int32, (rows, rows), 1)

    def column(values):
        spread = jnp.broadcast_to(values.astype(jnp.float32), (rows, rows))
        total = jnp.sum(jnp.where(diagonal, spread, 0.0), axis=1, keepdims=True)
        return jnp.broadcast_to(total.astype(jnp.int32), (rows, extra))

    every = []
    target = 0
    for step in range(steps_here):
        ids, gates = ids_ref[step], gates_ref[step]
        code = jnp.zeros((rows, extra), jnp.int32)
        for route in range(ids.shape[0]):
            code += jnp.where(column(ids[route : route + 1]) == expert, column(gates[route : route + 1]), 0)
        low = code & 15
        sent = jnp.where(lane < ep_count, code - low, jnp.where(lane < 2 * ep_count, low, 0))
        pieces = [sent.astype(jnp.float32)]
        scales = scales_ref[step]
        codes = codes_ref[step].astype(jnp.float32)
        for b in range(blocks):
            pieces.append(codes[:, b * size : (b + 1) * size] * jnp.broadcast_to(scales[:, b : b + 1], (rows, size)))
        row = jnp.concatenate(pieces, axis=1)
        every.append(row)
        for start, end in spans_of(features, cuts[step], extra):
            part_refs[target][...] = row[:, start:end].astype(jnp.bfloat16)
            target += 1
    all_ref[...] = jnp.concatenate(every, axis=0).astype(jnp.bfloat16)


def spans_of(features, count, extra):
    width = features // count
    return [(extra + k * width if k else 0, extra + (k + 1) * width) for k in range(count)]


def prepare(row_codes, row_scales, expert_ids, gate_codes, ep_count, cuts):
    steps_here, rows, features = row_codes.shape
    extra = -(-2 * ep_count // 128) * 128
    shapes = [jax.ShapeDtypeStruct((steps_here * rows, features + extra), jnp.bfloat16)]
    for step in range(steps_here):
        for start, end in spans_of(features, cuts[step], extra):
            shapes.append(jax.ShapeDtypeStruct((rows, end - start), jnp.bfloat16))
    ins = [row_codes, row_scales, expert_ids.transpose(0, 2, 1), gate_codes.transpose(0, 2, 1)]
    outs = pl.pallas_call(
        functools.partial(prepare_kernel, ep_count, extra, cuts),
        out_shape=shapes,
        in_specs=[pl.BlockSpec(memory_space=pl.ANY)] * len(ins),
        scratch_shapes=[pltpu.VMEM(v.shape, v.dtype) for v in ins] + [pltpu.SemaphoreType.DMA((len(ins),))],
    )(*ins)
    return outs[0], outs[1:], extra


def body(row_codes, row_scales, expert_ids, gate_codes, w_gate, w_up, w_down):
    ep_count = lax.axis_size("ep")
    sub_bits = bits_of(lax.axis_size("sub"))
    ep_bits = bits_of(ep_count)
    steps_here, rows, features = row_codes.shape
    out_cuts = [column_parts] + [F_OUT1] * (steps_here - 1)
    back_cuts = [F_BACK0] + [column_parts] * (steps_here - 1)
    tokens, owns, extra = prepare(row_codes, row_scales, expert_ids, gate_codes, ep_count, out_cuts)
    crossed = swap(tokens, "ep", ep_bits[0])
    me = lax.axis_index("ep")
    far, near, xs = [], [], []
    gathered = []
    for step in range(steps_here):
        parts = []
        for k, (start, end) in enumerate(spans_of(features, out_cuts[step], extra)):
            part = owns[len(xs)]
            for n, bit in enumerate(sub_bits):
                if n == 0 and step >= 1 and F_Z2 == 1:
                    part = after(part, near[0])
                if n == 0 and step >= 1 and F_Z2 == 2:
                    part = after(part, far[1])
                if n == 0 and step >= 1 and F_Z2 == 3:
                    part = after(part, far[0])
                came = swap(part, "sub", bit)
                if n == 0:
                    far.append(came)
                if n == 1:
                    near.append(came)
                part = join(part, came)
            give = part[rows:]
            if F_XORD and step >= 1:
                give = after(give, xs[F_XORD - 1])
            xs.append(swap(give, "ep", ep_bits[0]))
            parts.append((part, crossed[step * rows : (step + 1) * rows, start:end], xs[-1]))
        gathered.append(parts)
    step_done, core_back = [], []
    returned = []
    for step in range(steps_here):
        gate_value = up_value = 0.0
        for part, (start, end) in zip(gathered[step], spans_of(features, out_cuts[step], extra)):
            part, came_own, came_rest = part
            if F_LATE and step_done:
                came_rest = after(came_rest, *step_done)
            part = join(part, came_own, came_rest)
            for bit in ep_bits[1:]:
                part = after(part, *step_done) if F_C1 else part
                part = join(part, swap(part, "ep", bit))
            part = after(part, *core_back) if F_CHOLD else part
            if start == 0:
                sent = part[:, : 2 * ep_count].astype(jnp.float32)
                dense = sent[:, :ep_count] + sent[:, ep_count:]
                total = jnp.sum(dense, axis=1, keepdims=True)
                mine = jnp.sum(jnp.where(jnp.arange(ep_count) == me, dense, 0.0), axis=1, keepdims=True)
                weight = routed_scale * mine / total
                part = part[:, extra:]
            span = slice(max(start - extra, 0), end - extra)
            gate_value += jnp.dot(part, w_gate[0, span], preferred_element_type=jnp.float32)
            up_value += jnp.dot(part, w_up[0, span], preferred_element_type=jnp.float32)
        hidden = (jax.nn.silu(gate_value) * up_value).astype(jnp.bfloat16)
        step_done = []
        core_back = []
        for start, end in spans_of(features, back_cuts[step], 0):
            held = jnp.dot(hidden, w_down[0, :, start:end], preferred_element_type=jnp.float32)
            held = (held * weight).astype(jnp.bfloat16)
            step_done.append(held)
            for bit in reversed(ep_bits[1:]):
                half = held.shape[0] // 2
                held = add_up(held[:half], swap(held[half:], "ep", bit)).astype(jnp.bfloat16)
            core_back.append(held)
            returned.append((step, start, end, held))
    last = [held for step, _, _, held in returned if step == steps_here - 1]
    finals, own_gives, owns, restss, crossings = [], [], [], [], []
    for step in range(steps_here):
        split = rows if step >= F_OWN0 else 0
        own, rests, gives = [], [], []
        for _, start, end, held in [entry for entry in returned if entry[0] == step]:
            half = held.shape[0] // 2
            came = swap(held[half + split :], "ep", ep_bits[0])
            mine = [held[:rows]]
            if split:
                gives.append(held[half : half + rows])
            else:
                mine.append(came[:rows])
                came = came[rows:]
            crossings.append(came)
            rest = add_up(held[rows:half], came).astype(jnp.bfloat16)
            for n, bit in enumerate(reversed(sub_bits[1:])):
                half = (rest.shape[0] + rows) // 2
                give = rest[half - rows :]
                if step == 0 and n == 0 and F_Z2R in (2, 5):
                    give = after(give, *last)
                came = swap(give, "sub", bit)
                mine.append(came[:rows])
                rest = add_up(rest[: half - rows], came[rows:]).astype(jnp.bfloat16)
            own.append(mine)
            rests.append(rest)
        owns.append(own)
        restss.append(rests)
        if split:
            own_gives.append(jnp.concatenate(gives, axis=1))
    for step in range(steps_here):
        own, rests = owns[step], restss[step]
        if step == 0 or not F_SPLIT1:
            give = jnp.concatenate(rests, axis=1)
            if step == 0 and F_Z2R == 1:
                give = after(give, *last)
            if step == 0 and F_Z2R in (3, 5):
                give = after(give, crossings[back_cuts[0]])
            if step == 0 and F_Z2R == 4:
                give = after(give, crossings[-1])
            if step and F_FIN0:
                give = after(give, finals[step - 1])
            came = swap(give, "sub", sub_bits[0])
        else:
            came = jnp.concatenate([swap(give, "sub", sub_bits[0]) for give in rests], axis=1)
        own = jnp.concatenate([add_up(*mine) for mine in own], axis=1)
        finals.append(add_up(own, came) if step >= F_OWN0 else add_up(own, came).astype(jnp.bfloat16))
    crossed = swap(join(*own_gives), "ep", ep_bits[0])
    for n in range(len(own_gives)):
        step = steps_here - len(own_gives) + n
        finals[step] = add_up(finals[step], crossed[n * rows : (n + 1) * rows]).astype(jnp.bfloat16)
    return jnp.stack(finals)


def solution(mesh):
    rows = P(None, ("groups", "ep", "sub"), None)
    return jax.shard_map(
        body,
        mesh=mesh,
        in_specs=(rows, rows, rows, rows, P("ep", None, "sub"), P("ep", None, "sub"), P("ep", "sub", None)),
        out_specs=rows,
        check_vma=False,
    )
```

```python
import functools

import jax
import jax.numpy as jnp
from jax import lax
from jax.experimental import pallas as pl
from jax.experimental.pallas import tpu as pltpu
from jax.sharding import PartitionSpec as P

routed_scale = 2.5
column_parts = 2
F_Z2 = 0
F_XORD = 2
F_C1 = 1
F_Z2R = 2
F_CHOLD = 1
F_OUT1 = 2
F_FIN0 = 1
F_OWN0 = 0
F_LATE = 1
F_SPLIT1 = 1
F_BACK0 = 2


def bits_of(count):
    return [1 << b for b in reversed(range(count.bit_length() - 1))]


def swap(value, axis_name, bit):
    count = lax.axis_size(axis_name)
    return lax.ppermute(value, axis_name, [(i, i ^ bit) for i in range(count)])


def after(value, *others):
    return lax.optimization_barrier((value, *others))[0] if others else value


def join(*parts):
    return jnp.concatenate(parts, axis=0)


def add_up(*terms):
    total = terms[0].astype(jnp.float32)
    for term in terms[1:]:
        total = total + term.astype(jnp.float32)
    return total


def prepare_kernel(ep_count, extra, cuts, codes_hbm, scales_hbm, ids_hbm, gates_hbm, all_ref, *refs):
    part_refs, (codes_ref, scales_ref, ids_ref, gates_ref, sems) = refs[:-5], refs[-5:]
    moves = []
    for n, (source, target) in enumerate(
        [(codes_hbm, codes_ref), (scales_hbm, scales_ref), (ids_hbm, ids_ref), (gates_hbm, gates_ref)]
    ):
        moves.append(pltpu.make_async_copy(source, target, sems.at[n]))
        moves[-1].start()
    for move in moves:
        move.wait()
    steps_here, rows, features = codes_ref.shape
    blocks = scales_ref.shape[2]
    size = features // blocks
    lane = lax.broadcasted_iota(jnp.int32, (rows, extra), 1)
    expert = lax.rem(lane, ep_count)
    diagonal = lax.broadcasted_iota(jnp.int32, (rows, rows), 0) == lax.broadcasted_iota(jnp.int32, (rows, rows), 1)

    def column(values):
        spread = jnp.broadcast_to(values.astype(jnp.float32), (rows, rows))
        total = jnp.sum(jnp.where(diagonal, spread, 0.0), axis=1, keepdims=True)
        return jnp.broadcast_to(total.astype(jnp.int32), (rows, extra))

    every = []
    target = 0
    for step in range(steps_here):
        ids, gates = ids_ref[step], gates_ref[step]
        code = jnp.zeros((rows, extra), jnp.int32)
        for route in range(ids.shape[0]):
            code += jnp.where(column(ids[route : route + 1]) == expert, column(gates[route : route + 1]), 0)
        low = code & 15
        sent = jnp.where(lane < ep_count, code - low, jnp.where(lane < 2 * ep_count, low, 0))
        pieces = [sent.astype(jnp.float32)]
        scales = scales_ref[step]
        codes = codes_ref[step].astype(jnp.float32)
        for b in range(blocks):
            pieces.append(codes[:, b * size : (b + 1) * size] * jnp.broadcast_to(scales[:, b : b + 1], (rows, size)))
        row = jnp.concatenate(pieces, axis=1)
        every.append(row)
        for start, end in spans_of(features, cuts[step], extra):
            part_refs[target][...] = row[:, start:end].astype(jnp.bfloat16)
            target += 1
    all_ref[...] = jnp.concatenate(every, axis=0).astype(jnp.bfloat16)


def spans_of(features, count, extra):
    width = features // count
    return [(extra + k * width if k else 0, extra + (k + 1) * width) for k in range(count)]


def prepare(row_codes, row_scales, expert_ids, gate_codes, ep_count, cuts):
    steps_here, rows, features = row_codes.shape
    extra = -(-2 * ep_count // 128) * 128
    shapes = [jax.ShapeDtypeStruct((steps_here * rows, features + extra), jnp.bfloat16)]
    for step in range(steps_here):
        for start, end in spans_of(features, cuts[step], extra):
            shapes.append(jax.ShapeDtypeStruct((rows, end - start), jnp.bfloat16))
    ins = [row_codes, row_scales, expert_ids.transpose(0, 2, 1), gate_codes.transpose(0, 2, 1)]
    outs = pl.pallas_call(
        functools.partial(prepare_kernel, ep_count, extra, cuts),
        out_shape=shapes,
        in_specs=[pl.BlockSpec(memory_space=pl.ANY)] * len(ins),
        scratch_shapes=[pltpu.VMEM(v.shape, v.dtype) for v in ins] + [pltpu.SemaphoreType.DMA((len(ins),))],
    )(*ins)
    return outs[0], outs[1:], extra


def body(row_codes, row_scales, expert_ids, gate_codes, w_gate, w_up, w_down):
    ep_count = lax.axis_size("ep")
    sub_bits = bits_of(lax.axis_size("sub"))
    ep_bits = bits_of(ep_count)
    steps_here, rows, features = row_codes.shape
    out_cuts = [column_parts] + [F_OUT1] * (steps_here - 1)
    back_cuts = [F_BACK0] + [column_parts] * (steps_here - 1)
    tokens, owns, extra = prepare(row_codes, row_scales, expert_ids, gate_codes, ep_count, out_cuts)
    crossed = swap(tokens, "ep", ep_bits[0])
    me = lax.axis_index("ep")
    far, near, xs = [], [], []
    gathered = []
    for step in range(steps_here):
        parts = []
        for k, (start, end) in enumerate(spans_of(features, out_cuts[step], extra)):
            part = owns[len(xs)]
            for n, bit in enumerate(sub_bits):
                if n == 0 and step >= 1 and F_Z2 == 1:
                    part = after(part, near[0])
                if n == 0 and step >= 1 and F_Z2 == 2:
                    part = after(part, far[1])
                if n == 0 and step >= 1 and F_Z2 == 3:
                    part = after(part, far[0])
                came = swap(part, "sub", bit)
                if n == 0:
                    far.append(came)
                if n == 1:
                    near.append(came)
                part = join(part, came)
            give = part[rows:]
            if F_XORD and step >= 1:
                give = after(give, xs[F_XORD - 1])
            xs.append(swap(give, "ep", ep_bits[0]))
            parts.append((part, crossed[step * rows : (step + 1) * rows, start:end], xs[-1]))
        gathered.append(parts)
    step_done, core_back = [], []
    returned = []
    for step in range(steps_here):
        gate_value = up_value = 0.0
        for part, (start, end) in zip(gathered[step], spans_of(features, out_cuts[step], extra)):
            part, came_own, came_rest = part
            if F_LATE and step_done:
                came_rest = after(came_rest, *step_done)
            part = join(part, came_own, came_rest)
            for bit in ep_bits[1:]:
                part = after(part, *step_done) if F_C1 else part
                part = join(part, swap(part, "ep", bit))
            part = after(part, *core_back) if F_CHOLD else part
            if start == 0:
                sent = part[:, : 2 * ep_count].astype(jnp.float32)
                dense = sent[:, :ep_count] + sent[:, ep_count:]
                total = jnp.sum(dense, axis=1, keepdims=True)
                mine = jnp.sum(jnp.where(jnp.arange(ep_count) == me, dense, 0.0), axis=1, keepdims=True)
                weight = routed_scale * mine / total
                part = part[:, extra:]
            span = slice(max(start - extra, 0), end - extra)
            gate_value += jnp.dot(part, w_gate[0, span], preferred_element_type=jnp.float32)
            up_value += jnp.dot(part, w_up[0, span], preferred_element_type=jnp.float32)
        hidden = (jax.nn.silu(gate_value) * up_value).astype(jnp.bfloat16)
        step_done = []
        core_back = []
        for start, end in spans_of(features, back_cuts[step], 0):
            held = jnp.dot(hidden, w_down[0, :, start:end], preferred_element_type=jnp.float32)
            held = (held * weight).astype(jnp.bfloat16)
            step_done.append(held)
            for bit in reversed(ep_bits[1:]):
                half = held.shape[0] // 2
                held = add_up(held[:half], swap(held[half:], "ep", bit)).astype(jnp.bfloat16)
            core_back.append(held)
            returned.append((step, start, end, held))
    last = [held for step, _, _, held in returned if step == steps_here - 1]
    finals, own_gives, owns, restss, crossings = [], [], [], [], []
    for step in range(steps_here):
        split = rows if step >= F_OWN0 else 0
        own, rests, gives = [], [], []
        for _, start, end, held in [entry for entry in returned if entry[0] == step]:
            half = held.shape[0] // 2
            came = swap(held[half + split :], "ep", ep_bits[0])
            mine = [held[:rows]]
            if split:
                gives.append(held[half : half + rows])
            else:
                mine.append(came[:rows])
                came = came[rows:]
            crossings.append(came)
            rest = add_up(held[rows:half], came).astype(jnp.bfloat16)
            for n, bit in enumerate(reversed(sub_bits[1:])):
                half = (rest.shape[0] + rows) // 2
                give = rest[half - rows :]
                if step == 0 and n == 0 and F_Z2R in (2, 5):
                    give = after(give, *last)
                came = swap(give, "sub", bit)
                mine.append(came[:rows])
                rest = add_up(rest[: half - rows], came[rows:]).astype(jnp.bfloat16)
            own.append(mine)
            rests.append(rest)
        owns.append(own)
        restss.append(rests)
        if split:
            own_gives.append(jnp.concatenate(gives, axis=1))
    for step in range(steps_here):
        own, rests = owns[step], restss[step]
        if step == 0 or not F_SPLIT1:
            give = jnp.concatenate(rests, axis=1)
            if step == 0 and F_Z2R == 1:
                give = after(give, *last)
            if step == 0 and F_Z2R in (3, 5):
                give = after(give, crossings[back_cuts[0]])
            if step == 0 and F_Z2R == 4:
                give = after(give, crossings[-1])
            if step and F_FIN0:
                give = after(give, finals[step - 1])
            came = swap(give, "sub", sub_bits[0])
        else:
            came = jnp.concatenate([swap(give, "sub", sub_bits[0]) for give in rests], axis=1)
        own = jnp.concatenate([add_up(*mine) for mine in own], axis=1)
        finals.append(add_up(own, came) if step >= F_OWN0 else add_up(own, came).astype(jnp.bfloat16))
    crossed = swap(join(*own_gives), "ep", ep_bits[0])
    for n in range(len(own_gives)):
        step = steps_here - len(own_gives) + n
        finals[step] = add_up(finals[step], crossed[n * rows : (n + 1) * rows]).astype(jnp.bfloat16)
    return jnp.stack(finals)


def solution(mesh):
    rows = P(None, ("groups", "ep", "sub"), None)
    return jax.shard_map(
        body,
        mesh=mesh,
        in_specs=(rows, rows, rows, rows, P("ep", None, "sub"), P("ep", None, "sub"), P("ep", "sub", None)),
        out_specs=rows,
        check_vma=False,
    )
```

```python
import functools

import jax
import jax.numpy as jnp
from jax import lax
from jax.experimental import pallas as pl
from jax.experimental.pallas import tpu as pltpu
from jax.sharding import PartitionSpec as P

routed_scale = 2.5
column_parts = 2
F_Z2 = 2
F_XORD = 2
F_C1 = 1
F_Z2R = 5
F_CHOLD = 1
F_OUT1 = 2
F_FIN0 = 1
F_OWN0 = 0
F_LATE = 1
F_SPLIT1 = 1
F_BACK0 = 2


def bits_of(count):
    return [1 << b for b in reversed(range(count.bit_length() - 1))]


def swap(value, axis_name, bit):
    count = lax.axis_size(axis_name)
    return lax.ppermute(value, axis_name, [(i, i ^ bit) for i in range(count)])


def after(value, *others):
    return lax.optimization_barrier((value, *others))[0] if others else value


def join(*parts):
    return jnp.concatenate(parts, axis=0)


def add_up(*terms):
    total = terms[0].astype(jnp.float32)
    for term in terms[1:]:
        total = total + term.astype(jnp.float32)
    return total


def prepare_kernel(ep_count, extra, cuts, codes_hbm, scales_hbm, ids_hbm, gates_hbm, all_ref, *refs):
    part_refs, (codes_ref, scales_ref, ids_ref, gates_ref, sems) = refs[:-5], refs[-5:]
    moves = []
    for n, (source, target) in enumerate(
        [(codes_hbm, codes_ref), (scales_hbm, scales_ref), (ids_hbm, ids_ref), (gates_hbm, gates_ref)]
    ):
        moves.append(pltpu.make_async_copy(source, target, sems.at[n]))
        moves[-1].start()
    for move in moves:
        move.wait()
    steps_here, rows, features = codes_ref.shape
    blocks = scales_ref.shape[2]
    size = features // blocks
    lane = lax.broadcasted_iota(jnp.int32, (rows, extra), 1)
    expert = lax.rem(lane, ep_count)
    diagonal = lax.broadcasted_iota(jnp.int32, (rows, rows), 0) == lax.broadcasted_iota(jnp.int32, (rows, rows), 1)

    def column(values):
        spread = jnp.broadcast_to(values.astype(jnp.float32), (rows, rows))
        total = jnp.sum(jnp.where(diagonal, spread, 0.0), axis=1, keepdims=True)
        return jnp.broadcast_to(total.astype(jnp.int32), (rows, extra))

    every = []
    target = 0
    for step in range(steps_here):
        ids, gates = ids_ref[step], gates_ref[step]
        code = jnp.zeros((rows, extra), jnp.int32)
        for route in range(ids.shape[0]):
            code += jnp.where(column(ids[route : route + 1]) == expert, column(gates[route : route + 1]), 0)
        low = code & 15
        sent = jnp.where(lane < ep_count, code - low, jnp.where(lane < 2 * ep_count, low, 0))
        pieces = [sent.astype(jnp.float32)]
        scales = scales_ref[step]
        codes = codes_ref[step].astype(jnp.float32)
        for b in range(blocks):
            pieces.append(codes[:, b * size : (b + 1) * size] * jnp.broadcast_to(scales[:, b : b + 1], (rows, size)))
        row = jnp.concatenate(pieces, axis=1)
        every.append(row)
        for start, end in spans_of(features, cuts[step], extra):
            part_refs[target][...] = row[:, start:end].astype(jnp.bfloat16)
            target += 1
    all_ref[...] = jnp.concatenate(every, axis=0).astype(jnp.bfloat16)


def spans_of(features, count, extra):
    width = features // count
    return [(extra + k * width if k else 0, extra + (k + 1) * width) for k in range(count)]


def prepare(row_codes, row_scales, expert_ids, gate_codes, ep_count, cuts):
    steps_here, rows, features = row_codes.shape
    extra = -(-2 * ep_count // 128) * 128
    shapes = [jax.ShapeDtypeStruct((steps_here * rows, features + extra), jnp.bfloat16)]
    for step in range(steps_here):
        for start, end in spans_of(features, cuts[step], extra):
            shapes.append(jax.ShapeDtypeStruct((rows, end - start), jnp.bfloat16))
    ins = [row_codes, row_scales, expert_ids.transpose(0, 2, 1), gate_codes.transpose(0, 2, 1)]
    outs = pl.pallas_call(
        functools.partial(prepare_kernel, ep_count, extra, cuts),
        out_shape=shapes,
        in_specs=[pl.BlockSpec(memory_space=pl.ANY)] * len(ins),
        scratch_shapes=[pltpu.VMEM(v.shape, v.dtype) for v in ins] + [pltpu.SemaphoreType.DMA((len(ins),))],
    )(*ins)
    return outs[0], outs[1:], extra


def body(row_codes, row_scales, expert_ids, gate_codes, w_gate, w_up, w_down):
    ep_count = lax.axis_size("ep")
    sub_bits = bits_of(lax.axis_size("sub"))
    ep_bits = bits_of(ep_count)
    steps_here, rows, features = row_codes.shape
    out_cuts = [column_parts] + [F_OUT1] * (steps_here - 1)
    back_cuts = [F_BACK0] + [column_parts] * (steps_here - 1)
    tokens, owns, extra = prepare(row_codes, row_scales, expert_ids, gate_codes, ep_count, out_cuts)
    crossed = swap(tokens, "ep", ep_bits[0])
    me = lax.axis_index("ep")
    far, near, xs = [], [], []
    gathered = []
    for step in range(steps_here):
        parts = []
        for k, (start, end) in enumerate(spans_of(features, out_cuts[step], extra)):
            part = owns[len(xs)]
            for n, bit in enumerate(sub_bits):
                if n == 0 and step >= 1 and F_Z2 == 1:
                    part = after(part, near[0])
                if n == 0 and step >= 1 and F_Z2 == 2:
                    part = after(part, far[1])
                if n == 0 and step >= 1 and F_Z2 == 3:
                    part = after(part, far[0])
                came = swap(part, "sub", bit)
                if n == 0:
                    far.append(came)
                if n == 1:
                    near.append(came)
                part = join(part, came)
            give = part[rows:]
            if F_XORD and step >= 1:
                give = after(give, xs[F_XORD - 1])
            xs.append(swap(give, "ep", ep_bits[0]))
            parts.append((part, crossed[step * rows : (step + 1) * rows, start:end], xs[-1]))
        gathered.append(parts)
    step_done, core_back = [], []
    returned = []
    for step in range(steps_here):
        gate_value = up_value = 0.0
        for part, (start, end) in zip(gathered[step], spans_of(features, out_cuts[step], extra)):
            part, came_own, came_rest = part
            if F_LATE and step_done:
                came_rest = after(came_rest, *step_done)
            part = join(part, came_own, came_rest)
            for bit in ep_bits[1:]:
                part = after(part, *step_done) if F_C1 else part
                part = join(part, swap(part, "ep", bit))
            part = after(part, *core_back) if F_CHOLD else part
            if start == 0:
                sent = part[:, : 2 * ep_count].astype(jnp.float32)
                dense = sent[:, :ep_count] + sent[:, ep_count:]
                total = jnp.sum(dense, axis=1, keepdims=True)
                mine = jnp.sum(jnp.where(jnp.arange(ep_count) == me, dense, 0.0), axis=1, keepdims=True)
                weight = routed_scale * mine / total
                part = part[:, extra:]
            span = slice(max(start - extra, 0), end - extra)
            gate_value += jnp.dot(part, w_gate[0, span], preferred_element_type=jnp.float32)
            up_value += jnp.dot(part, w_up[0, span], preferred_element_type=jnp.float32)
        hidden = (jax.nn.silu(gate_value) * up_value).astype(jnp.bfloat16)
        step_done = []
        core_back = []
        for start, end in spans_of(features, back_cuts[step], 0):
            held = jnp.dot(hidden, w_down[0, :, start:end], preferred_element_type=jnp.float32)
            held = (held * weight).astype(jnp.bfloat16)
            step_done.append(held)
            for bit in reversed(ep_bits[1:]):
                half = held.shape[0] // 2
                held = add_up(held[:half], swap(held[half:], "ep", bit)).astype(jnp.bfloat16)
            core_back.append(held)
            returned.append((step, start, end, held))
    last = [held for step, _, _, held in returned if step == steps_here - 1]
    finals, own_gives, owns, restss, crossings = [], [], [], [], []
    for step in range(steps_here):
        split = rows if step >= F_OWN0 else 0
        own, rests, gives = [], [], []
        for _, start, end, held in [entry for entry in returned if entry[0] == step]:
            half = held.shape[0] // 2
            came = swap(held[half + split :], "ep", ep_bits[0])
            mine = [held[:rows]]
            if split:
                gives.append(held[half : half + rows])
            else:
                mine.append(came[:rows])
                came = came[rows:]
            crossings.append(came)
            rest = add_up(held[rows:half], came).astype(jnp.bfloat16)
            for n, bit in enumerate(reversed(sub_bits[1:])):
                half = (rest.shape[0] + rows) // 2
                give = rest[half - rows :]
                if step == 0 and n == 0 and F_Z2R in (2, 5):
                    give = after(give, *last)
                came = swap(give, "sub", bit)
                mine.append(came[:rows])
                rest = add_up(rest[: half - rows], came[rows:]).astype(jnp.bfloat16)
            own.append(mine)
            rests.append(rest)
        owns.append(own)
        restss.append(rests)
        if split:
            own_gives.append(jnp.concatenate(gives, axis=1))
    for step in range(steps_here):
        own, rests = owns[step], restss[step]
        if step == 0 or not F_SPLIT1:
            give = jnp.concatenate(rests, axis=1)
            if step == 0 and F_Z2R == 1:
                give = after(give, *last)
            if step == 0 and F_Z2R in (3, 5):
                give = after(give, crossings[back_cuts[0]])
            if step == 0 and F_Z2R == 4:
                give = after(give, crossings[-1])
            if step and F_FIN0:
                give = after(give, finals[step - 1])
            came = swap(give, "sub", sub_bits[0])
        else:
            came = jnp.concatenate([swap(give, "sub", sub_bits[0]) for give in rests], axis=1)
        own = jnp.concatenate([add_up(*mine) for mine in own], axis=1)
        finals.append(add_up(own, came) if step >= F_OWN0 else add_up(own, came).astype(jnp.bfloat16))
    crossed = swap(join(*own_gives), "ep", ep_bits[0])
    for n in range(len(own_gives)):
        step = steps_here - len(own_gives) + n
        finals[step] = add_up(finals[step], crossed[n * rows : (n + 1) * rows]).astype(jnp.bfloat16)
    return jnp.stack(finals)


def solution(mesh):
    rows = P(None, ("groups", "ep", "sub"), None)
    return jax.shard_map(
        body,
        mesh=mesh,
        in_specs=(rows, rows, rows, rows, P("ep", None, "sub"), P("ep", None, "sub"), P("ep", "sub", None)),
        out_specs=rows,
        check_vma=False,
    )
```
